128 devices in a mesh: dp: 4 (over z_lo, core), eig: 32 (over z_hi, y, x).
Axes of the slice: x: 4, y: 4, z: 4 (z_hi: 2, z_lo: 2; z = z_hi * 2 + z_lo), core: 2. Of those that a mesh axis runs over, the one named last changes fastest.
Arguments:
- acts: bfloat16 [16, 256, 4096], P('dp', 'eig'), may hold values from -6 to 6
- grads: bfloat16 [16, 256, 11008], P('dp', 'eig'), may hold values from -0.375 to 0.375
- basis_in: bfloat16 [4096, 4096], P(None, 'eig'), may hold values from -0.09375 to 0.09375
- basis_out: bfloat16 [11008, 11008], P(None, 'eig'), may hold values from -0.0546875 to 0.0546875
Outputs:
- correction: float32 [11008, 4096], P('eig', 'dp')
The draws below stay inside these ranges and needn't reach their ends.
All inputs are finite; a program needn't handle non-finite values.
Results may differ from the reference program's by a relative error of at most 0.002.
Values may be sent and summed in bfloat16 or wider, within the bound.
No kernel may reach another device: no remote copies, remote signals or barrier semaphores. Data moves between devices by JAX's collectives and lax.ppermute only.
A program may use at most 128 MiB of HBM per device.

```python
import jax
import jax.numpy as jnp

D = 4096
FF = 11008
SEQ = 256
EXAMPLES = 16


def steps_of(stream_key, extent, split, low, largest):
    def one(position, parts):
        heights = jax.random.uniform(jax.random.fold_in(jax.random.fold_in(stream_key, 6), position), (parts,), jnp.float32, low / len(split), largest / len(split))
        return jnp.repeat(jnp.exp(heights), extent[position] // parts).reshape((-1,) + (1,) * (len(extent) - position - 1))

    factor_of = one(*split[0])
    for cut in split[1:]:
        factor_of = factor_of * one(*cut)
    return factor_of


def bell_draw(stream_key, shape, width, most, cuts=(), held_as=jnp.bfloat16):
    result = width * jax.random.normal(stream_key, shape, jnp.float32)
    if cuts:
        result = result * steps_of(stream_key, shape, cuts, -0.22, 0.18)
    return jnp.clip(result, -most, most).astype(held_as)


def setup_inputs(seed: int = 0) -> dict:
    arg_keys = jax.random.split(jax.random.key(seed), 5)
    return {
        "acts": bell_draw(arg_keys[0], (EXAMPLES, SEQ, D), 1.0, 6.0, ((0, 4), (1, 32))),
        "grads": bell_draw(arg_keys[1], (EXAMPLES, SEQ, FF), SEQ ** -0.5, 0.375, ((0, 4), (1, 32))),
        "basis_in": bell_draw(arg_keys[2], (D, D), D ** -0.5, 0.09375, ((1, 32),)),
        "basis_out": bell_draw(arg_keys[3], (FF, FF), FF ** -0.5, 0.0546875, ((1, 32),)),
    }


def reference(acts, grads, basis_in, basis_out):
    rot_acts = jnp.einsum("esd,dk->esk", acts.astype(jnp.float32), basis_in.astype(jnp.float32)).astype(jnp.bfloat16)
    rot_grads = jnp.einsum("esf,fk->esk", grads.astype(jnp.float32), basis_out.astype(jnp.float32)).astype(jnp.bfloat16)
    total = jnp.zeros((FF, D), jnp.float32)
    for number in range(EXAMPLES):
        product = jnp.dot(rot_grads[number].T, rot_acts[number], preferred_element_type=jnp.float32)
        total = total + product * product
    return total / EXAMPLES
```

```python
import jax
import jax.numpy as jnp
from jax import lax
from jax.experimental import pallas as pl
from jax.experimental.pallas import tpu as pltpu
from jax.sharding import Mesh
from jax.sharding import PartitionSpec as P

AXES = ("zl", "c", "zh", "y", "x")


def near_pairs(axis, step):
    masks = ((1, 3), (3, 1))
    table = [
        (core * 4 + i, core * 4 + (i ^ masks[core][step])) for core in range(2) for i in range(4)
    ]
    return lambda v: lax.ppermute(v, ("c", axis), table)


def order_of(half):
    first, second = ("x", "y") if half == 0 else ("y", "x")
    return ((first, 0), (first, 1), (second, 0), (second, 1))


def flip_zh(v):
    return lax.ppermute(v, "zh", [(0, 1), (1, 0)])


def flip_zl(v):
    return lax.ppermute(v, "zl", [(0, 1), (1, 0)])


def flip_both(v):
    return lax.ppermute(v, ("zl", "zh"), [(i, 3 - i) for i in range(4)])


def flip_core(v):
    return lax.ppermute(v, "c", [(0, 1), (1, 0)])


def turned(v, axis, core):
    size = v.shape[axis] // 2
    parts = [lax.dynamic_slice_in_dim(v, start * size, size, axis) for start in (core, 1 - core)]
    return jnp.concatenate(parts, axis)


def gather_tokens(v, half):
    for axis, step in order_of(half):
        v = jnp.concatenate([v, near_pairs(axis, step)(v)], 1)
    return v


def gather_columns(v, half):
    examples, tokens, columns = v.shape
    swapped = v.reshape(examples, tokens // 16, 2, 8, columns)[:, :, ::-1].reshape(v.shape)
    (axis, step), *rest = order_of(half)
    v = jnp.stack([v, near_pairs(axis, step)(swapped)])
    for axis, step in rest[:-1]:
        v = jnp.concatenate([v, near_pairs(axis, step)(v)], 0)
    axis, step = rest[-1]
    return v, near_pairs(axis, step)(v)


def product_kernel(place_ref, *refs):
    lefts, rights, out_ref = refs[:8], refs[8:12], refs[12]
    def left(half, group, example):
        pair = [lefts[half * 4 + group * 2 + i] for i in range(2)]
        return jnp.concatenate([r[:, example * 128 : (example + 1) * 128] for r in pair], 1)

    def right(half, piece, example):
        ref = rights[half * 2 + piece // 8]
        tiles = []
        for side in range(2):
            for u in range(8):
                row = side * 128 + (u ^ (piece >> 1)) * 16
                tiles.append(ref[piece % 8, example, row : row + 16, :])
        return jnp.concatenate(tiles, 0)

    for pair in range(8):
        sources = (2 * pair, 2 * pair + 1)
        total = None
        for half in range(2):
            pieces = [s if half == 0 else (s % 4) * 4 + s // 4 for s in sources]
            for group in range(2):
                for example in range(2):
                    rhs = jnp.concatenate(
                        [right(half, piece, group * 2 + example) for piece in pieces], 1
                    )
                    product = jnp.dot(
                        left(half, group, example), rhs, preferred_element_type=jnp.float32
                    )
                    square = product * product
                    total = square if total is None else total + square
        total = total * (1.0 / 16.0)
        for i, s in enumerate(sources):
            place = place_ref[s]
            column = pl.multiple_of(lax.rem(place, 8) * 128, 128)
            out_ref[place // 8, :, pl.ds(column, 128)] = total[:, i * 128 : (i + 1) * 128]


def product(places, lefts, rights):
    rows = lefts[0].shape[0]
    vmem = pl.BlockSpec(memory_space=pltpu.VMEM)
    return pl.pallas_call(
        product_kernel,
        out_shape=jax.ShapeDtypeStruct((2, rows, 1024), jnp.float32),
        in_specs=[pl.BlockSpec(memory_space=pltpu.SMEM)] + [vmem] * 12,
        out_specs=vmem,
        compiler_params=pltpu.CompilerParams(vmem_limit_bytes=40 * 1024 * 1024),
        cost_estimate=pl.CostEstimate(
            flops=2 * 8 * 256 * rows * 2048, bytes_accessed=14_000_000, transcendentals=0
        ),
        name="squares",
    )(places, *lefts, *rights)


def per_device(acts, grads, basis_in, basis_out):
    core, zl, zh = lax.axis_index("c"), lax.axis_index("zl"), lax.axis_index("zh")
    y, x = lax.axis_index("y"), lax.axis_index("x")

    acts = turned(acts, 2, core)
    basis_in = turned(basis_in, 0, core)
    part = flip_both(basis_in[:2048])
    other_in = jnp.concatenate([part, flip_core(part)], 0)
    own_acts = [gather_tokens(acts[2 * h : 2 * h + 2], h) for h in range(2)]

    grads = turned(grads, 2, core)
    basis_out = turned(basis_out, 0, core)
    part = flip_both(basis_out[:5504])
    other_out = jnp.concatenate([part, flip_core(part)], 0)
    own_grads = [gather_tokens(grads[2 * h : 2 * h + 2], h) for h in range(2)]

    def rotate(tokens, basis):
        return jnp.einsum(
            "esd,dk->esk", tokens, basis, preferred_element_type=jnp.float32
        ).astype(jnp.bfloat16)

    def rotate_turned(tokens, basis):
        return jnp.einsum(
            "esf,fk->kes", tokens, basis, preferred_element_type=jnp.float32
        ).astype(jnp.bfloat16).reshape(basis.shape[1], -1)

    rights = []
    for h in range(2):
        both = rotate(own_acts[h], jnp.concatenate([basis_in, other_in], 1))
        mine, theirs = both[..., :128], both[..., 128:]
        same = zh == zl
        keep, give = jnp.where(same, mine, theirs), jnp.where(same, theirs, mine)
        columns = jnp.concatenate(
            [
                jnp.concatenate([keep, flip_zh(keep)], 1),
                jnp.concatenate([flip_zl(give), flip_both(give)], 1),
            ],
            0,
        )
        rights += list(gather_columns(columns, h))

    lefts = []
    for h in range(2):
        mine = rotate_turned(own_grads[h], basis_out)
        theirs = rotate_turned(own_grads[h], other_out)
        lefts += [mine, flip_zh(theirs), flip_zl(mine), flip_both(theirs)]

    low, high = jnp.where(core == 0, 1, 3), jnp.where(core == 0, 3, 1)

    def mask(bits):
        return (low if bits & 1 else 0) ^ (high if bits & 2 else 0)

    places = jnp.stack(
        [((y ^ mask(s // 4)) * 4 + (x ^ mask(s % 4))) ^ (core * 8) for s in range(16)]
    ).astype(jnp.int32)
    sums = product(places, lefts, rights)
    return sums[0] + flip_core(sums[1])


def solution(mesh):
    fine = Mesh(mesh.devices.reshape(2, 2, 2, 4, 4), AXES)
    dp, eig = ("zl", "c"), ("zh", "y", "x")
    placed = (P(dp, eig, None), P(dp, eig, None), P(None, eig), P(None, eig))
    return jax.shard_map(
        per_device, mesh=fine, in_specs=placed, out_specs=P(eig, dp), check_vma=False
    )
```

```python
import jax
import jax.numpy as jnp
from jax import lax
from jax.experimental import pallas as pl
from jax.experimental.pallas import tpu as pltpu
from jax.sharding import Mesh
from jax.sharding import PartitionSpec as P

AXES = ("zl", "c", "zh", "y", "x")
ROOM = 56 * 1024 * 1024
CUTS = ((0, 2816), (2816, 2688))


def relay(v, hops):
    table = []
    for core, hop in enumerate(hops):
        for zl in range(2):
            for zh in range(2):
                to = {"both": (1 - zl, 1 - zh), "zl": (1 - zl, zh)}.get(hop)
                if to:
                    table.append((zl * 4 + core * 2 + zh, to[0] * 4 + core * 2 + to[1]))
    return lax.ppermute(v, ("zl", "c", "zh"), table)


def near_pairs(axis, step):
    masks = ((1, 3), (3, 1))
    table = [
        (core * 4 + i, core * 4 + (i ^ masks[core][step])) for core in range(2) for i in range(4)
    ]
    return lambda v: lax.ppermute(v, ("c", axis), table)


def steps_of(half):
    first, second = ("x", "y") if half == 0 else ("y", "x")
    return [near_pairs(axis, step) for axis in (first, second) for step in range(2)]


def flip_zh(v):
    return lax.ppermute(v, "zh", [(0, 1), (1, 0)])


def flip_zl(v):
    return lax.ppermute(v, "zl", [(0, 1), (1, 0)])


def flip_both(v):
    return lax.ppermute(v, ("zl", "zh"), [(i, 3 - i) for i in range(4)])


def flip_core(v):
    return lax.ppermute(v, "c", [(0, 1), (1, 0)])


def after(v, *others):
    return lax.optimization_barrier((v, *others))[0]


def rotate_in_kernel(flag_ref, *refs):
    tokens, own, other, (keep_ref, give_ref) = refs[:4], refs[4], refs[5], refs[6:]
    total = None
    for start in range(0, 4096, 512):
        lhs = jnp.concatenate(
            [
                tokens[half * 2 + piece][example, :, start : start + 512]
                for half in range(2)
                for example in range(2)
                for piece in range(2)
            ],
            0,
        )
        rhs = jnp.concatenate([own[start : start + 512, :], other[start : start + 512, :]], 1)
        part = jnp.dot(lhs, rhs, preferred_element_type=jnp.float32)
        total = part if total is None else total + part
    total = total.astype(jnp.bfloat16)
    mine, theirs = total[:, :128], total[:, 128:]

    @pl.when(flag_ref[0] == 1)
    def _():
        keep_ref[...] = mine
        give_ref[...] = theirs

    @pl.when(flag_ref[0] == 0)
    def _():
        keep_ref[...] = theirs
        give_ref[...] = mine


def rotate_in(flag, tokens, own, other):
    vmem = pl.BlockSpec(memory_space=pltpu.VMEM)
    shape = jax.ShapeDtypeStruct((512, 128), jnp.bfloat16)
    return pl.pallas_call(
        rotate_in_kernel,
        out_shape=(shape, shape),
        in_specs=[pl.BlockSpec(memory_space=pltpu.SMEM)] + [vmem] * 6,
        out_specs=(vmem, vmem),
        compiler_params=pltpu.CompilerParams(vmem_limit_bytes=ROOM),
        cost_estimate=pl.CostEstimate(
            flops=2 * 512 * 256 * 4096, bytes_accessed=6_500_000, transcendentals=0
        ),
        name="rotate_in",
    )(flag, *tokens, own, other)


def rotate_out_kernel(place_ref, *refs):
    tokens, refs = refs[:4], refs[4:]
    (basis, out_ref, refs) = (refs[:1], refs[1], refs[2:]) if len(refs) == 7 else (refs[:4], refs[4], refs[5:])
    kept_basis, kept_tokens, sems = refs[:2], refs[2:4], refs[4]
    copies = []
    for i in range(2):
        for start, size in CUTS:
            lanes = slice(start, start + size)
            offset = pl.multiple_of(place_ref[i] + start, 128)
            if len(basis) == 1:
                source = basis[0].at[:, i * 5504 + start : i * 5504 + start + size]
                group = [(source, kept_basis[i].at[:, lanes])]
            else:
                rows = [pl.multiple_of(place_ref[2 + 2 * i + j], 16) for j in range(2)]
                group = [
                    (basis[2 * i + j].at[:, lanes], kept_basis[i].at[pl.ds(rows[j], 176), lanes])
                    for j in range(2)
                ]
            for half in range(2):
                for piece in range(2):
                    group.append(
                        (
                            tokens[half * 2 + piece].at[:, :, pl.ds(offset, size)],
                            kept_tokens[i].at[
                                half * 2 : half * 2 + 2, piece * 64 : piece * 64 + 64, lanes
                            ],
                        )
                    )
            copies.append(
                [
                    pltpu.make_async_copy(source, target, sems.at[6 * len(copies) + j])
                    for j, (source, target) in enumerate(group)
                ]
            )
    for group in copies:
        for copy in group:
            copy.start()
    total = [None, None]
    for i, group in enumerate(copies):
        for copy in group:
            copy.wait()
        start, size = CUTS[i % 2]
        lanes = slice(start, start + size)
        for half in range(2):
            part = lax.dot_general(
                kept_basis[i // 2][:, lanes],
                kept_tokens[i // 2][half * 2 : half * 2 + 2, :, lanes].reshape(256, size),
                (((1,), (1,)), ((), ())),
                preferred_element_type=jnp.float32,
            )
            total[half] = part if total[half] is None else total[half] + part
    for half in range(2):
        rows = total[half]
        if len(basis) > 1:
            swap = place_ref[6] == 0
            low, high = rows[:176], rows[176:]
            rows = jnp.concatenate(
                [jnp.where(swap, low, high), jnp.where(swap, high, low)[8:]], 0
            )
        out_ref[:, half * 256 : half * 256 + 256] = rows.astype(out_ref.dtype)


def rotate_out(places, tokens, basis, name):
    rows = 344 if len(basis) == 1 else 352
    anywhere = pl.BlockSpec(memory_space=pltpu.HBM)
    return pl.pallas_call(
        rotate_out_kernel,
        out_shape=jax.ShapeDtypeStruct((344, 512), jnp.bfloat16),
        in_specs=[pl.BlockSpec(memory_space=pltpu.SMEM)] + [anywhere] * (4 + len(basis)),
        out_specs=pl.BlockSpec(memory_space=pltpu.VMEM),
        scratch_shapes=[pltpu.VMEM((rows, 5504), jnp.bfloat16)] * 2
        + [pltpu.VMEM((4, 128, 5504), jnp.bfloat16)] * 2
        + [pltpu.SemaphoreType.DMA((24,))],
        compiler_params=pltpu.CompilerParams(vmem_limit_bytes=ROOM),
        cost_estimate=pl.CostEstimate(
            flops=2 * 512 * rows * 11008, bytes_accessed=(512 + rows) * 22016, transcendentals=0
        ),
        name=name,
    )(places, *tokens, *basis)


def product_kernel(place_ref, *refs):
    lefts, rights, (keep_ref, give_ref) = refs[:4], refs[4:12], refs[12:]

    def left(half, group, example):
        lane = (half * 2 + example) * 128
        pair = [lefts[group * 2 + i] for i in range(2)]
        return jnp.concatenate([r[:, lane : lane + 128] for r in pair], 1)

    def right(half, piece, example):
        ref = rights[half * 4 + piece // 4]
        tiles = []
        for side in range(2):
            for u in range(8):
                row = side * 128 + (u ^ (piece >> 1)) * 16
                tiles.append(ref[piece % 4, example, row : row + 16, :])
        return jnp.concatenate(tiles, 0)

    for pair in range(8):
        sources = (2 * pair, 2 * pair + 1)
        total = None
        for half in range(2):
            pieces = [s if half == 0 else (s % 4) * 4 + s // 4 for s in sources]
            for group in range(2):
                for example in range(2):
                    rhs = jnp.concatenate(
                        [right(half, piece, group * 2 + example) for piece in pieces], 1
                    )
                    product = jnp.dot(
                        left(half, group, example), rhs, preferred_element_type=jnp.float32
                    )
                    square = product * product
                    total = square if total is None else total + square
        total = total * (1.0 / 16.0)
        for i, s in enumerate(sources):
            place = place_ref[s]
            column = pl.multiple_of(lax.rem(place, 8) * 128, 128)
            part = total[:, i * 128 : (i + 1) * 128]

            @pl.when(place < 8)
            def _(part=part, column=column):
                keep_ref[:, pl.ds(column, 128)] = part

            @pl.when(place >= 8)
            def _(part=part, column=column):
                give_ref[:, pl.ds(column, 128)] = part


def product(places, lefts, rights):
    rows = lefts[0].shape[0]
    shape = jax.ShapeDtypeStruct((rows, 1024), jnp.float32)
    vmem = pl.BlockSpec(memory_space=pltpu.VMEM)
    return pl.pallas_call(
        product_kernel,
        out_shape=(shape, shape),
        in_specs=[pl.BlockSpec(memory_space=pltpu.SMEM)] + [vmem] * 12,
        out_specs=(vmem, vmem),
        compiler_params=pltpu.CompilerParams(vmem_limit_bytes=24 * 1024 * 1024),
        cost_estimate=pl.CostEstimate(
            flops=2 * 8 * 256 * rows * 2048, bytes_accessed=14_000_000, transcendentals=0
        ),
        name="squares",
    )(places, *lefts, *rights)


def per_device(acts, grads, basis_in, basis_out):
    core, zl, zh = lax.axis_index("c"), lax.axis_index("zl"), lax.axis_index("zh")
    y, x = lax.axis_index("y"), lax.axis_index("x")
    steps = [steps_of(half) for half in range(2)]
    halves = range(2)

    def moved(v, step, *others):
        return [steps[half][step](after(v[half], *others) if others else v[half]) for half in halves]

    def joined(v, w, axis):
        return [jnp.concatenate([v[half], w[half]], axis) for half in halves]

    basis_out = basis_out.T

    a0 = [acts[2 * half : 2 * half + 2] for half in halves]
    g0 = [grads[2 * half : 2 * half + 2] for half in halves]
    a1 = joined(a0, moved(a0, 0), 1)
    other_in = flip_both(basis_in)
    window = lax.dynamic_slice(basis_out, (168 * (1 - zl), 5504 * core), (176, 5504))
    g1 = joined(g0, moved(g0, 0), 1)
    a2 = joined(a1, moved(a1, 1), 1)
    first = relay(after(window, other_in), ("both", None))
    g2 = joined(g1, moved(g1, 1), 1)
    a3 = joined(a2, moved(a2, 2), 1)
    a4 = moved(a3, 3)

    flag = (zh == zl).astype(jnp.int32).reshape(1)
    acts_pieces = [a3[0], a4[0], a3[1], a4[1]]
    keep, give = rotate_in(after(flag, first, *g2), acts_pieces, basis_in, other_in)
    keep, give = keep.reshape(4, 128, 128), give.reshape(4, 128, 128)
    exchanged = flip_zh(keep), flip_zl(give), flip_both(give)
    g3 = joined(g2, moved(g2, 2), 1)
    g4 = moved(g3, 3)
    near = jnp.concatenate([keep, exchanged[0]], 1)
    far = jnp.concatenate(exchanged[1:], 1)

    c0 = [
        jnp.concatenate([near[2 * half : 2 * half + 2], far[2 * half : 2 * half + 2]], 0)
        for half in halves
    ]
    swapped = [v.reshape(4, 16, 2, 8, 128)[:, :, ::-1].reshape(4, 256, 128) for v in c0]
    c1 = [jnp.stack([c0[half], v]) for half, v in enumerate(moved(swapped, 0, *g3))]
    second = relay(after(jnp.where(core == 0, first, window), *exchanged), ("zl", "both"))
    third = relay(after(second, *c1, *g4), (None, "zl"))

    grads_pieces = [v[half] for half in halves for v in (g3, g4)]
    places = jnp.array([0, 5504], jnp.int32)
    mine = rotate_out(places, grads_pieces, [basis_out], "rotate_own")
    c2 = joined(c1, [after(v, mine) for v in moved(c1, 1, *g4)], 0)
    c3 = moved(c2, 2)
    c4 = moved(c2, 3)
    c5 = moved(c3, 3)
    rights = [v[half] for half in halves for v in (c2, c3, c4, c5)]
    outer = jnp.where(core == 0, first, third)
    places = [5504 * core, 5504 * (1 - core)]
    places += [176 * core, 176 * (1 - core), 176 * core, 176 * (1 - core), zl]
    theirs = rotate_out(
        jnp.stack(places).astype(jnp.int32),
        grads_pieces,
        [outer, second, flip_core(after(second, *c2)), flip_core(after(outer, *c3, *c4))],
        "rotate_other",
    )
    lefts = [mine, flip_zh(theirs), flip_zl(mine), flip_both(theirs)]

    low, high = jnp.where(core == 0, 1, 3), jnp.where(core == 0, 3, 1)

    def mask(bits):
        return (low if bits & 1 else 0) ^ (high if bits & 2 else 0)

    places = jnp.stack(
        [((y ^ mask(s // 4)) * 4 + (x ^ mask(s % 4))) ^ (core * 8) for s in range(16)]
    ).astype(jnp.int32)
    keep, give = product(places, lefts, rights)
    return keep + flip_core(give)


def solution(mesh):
    fine = Mesh(mesh.devices.reshape(2, 2, 2, 4, 4), AXES)
    dp, eig = ("zl", "c"), ("zh", "y", "x")
    placed = (P(dp, eig, None), P(dp, eig, None), P(None, eig), P(None, eig))
    return jax.shard_map(
        per_device, mesh=fine, in_specs=placed, out_specs=P(eig, dp), check_vma=False
    )
```

```python
import jax
import jax.numpy as jnp
from jax import lax
from jax.experimental import pallas as pl
from jax.experimental.pallas import tpu as pltpu
from jax.sharding import Mesh
from jax.sharding import PartitionSpec as P

AXES = ("zl", "c", "zh", "y", "x")
ROOM = 56 * 1024 * 1024
CUTS = ((0, 2816), (2816, 2688))


def relay(v, hops):
    table = []
    for core, hop in enumerate(hops):
        for zl in range(2):
            for zh in range(2):
                to = {"both": (1 - zl, 1 - zh), "zl": (1 - zl, zh)}.get(hop)
                if to:
                    table.append((zl * 4 + core * 2 + zh, to[0] * 4 + core * 2 + to[1]))
    return lax.ppermute(v, ("zl", "c", "zh"), table)


def near_pairs(axis, step):
    masks = ((1, 3), (3, 1))
    table = [
        (core * 4 + i, core * 4 + (i ^ masks[core][step])) for core in range(2) for i in range(4)
    ]
    return lambda v: lax.ppermute(v, ("c", axis), table)


def steps_of(half):
    first, second = ("x", "y") if half == 0 else ("y", "x")
    return [near_pairs(axis, step) for axis in (first, second) for step in range(2)]


def flip_zh(v):
    return lax.ppermute(v, "zh", [(0, 1), (1, 0)])


def flip_zl(v):
    return lax.ppermute(v, "zl", [(0, 1), (1, 0)])


def flip_both(v):
    return lax.ppermute(v, ("zl", "zh"), [(i, 3 - i) for i in range(4)])


def flip_core(v):
    return lax.ppermute(v, "c", [(0, 1), (1, 0)])


def after(v, *others):
    return lax.optimization_barrier((v, *others))[0]


def rotate_in_kernel(flag_ref, *refs):
    tokens, own, (near, far), (keep_ref, give_ref) = refs[:4], refs[4], refs[5:7], refs[7:]
    total = None
    for start in range(0, 4096, 512):
        lhs = jnp.concatenate(
            [
                tokens[half * 2 + piece][example, :, start : start + 512]
                for half in range(2)
                for example in range(2)
                for piece in range(2)
            ],
            0,
        )
        rows = slice(start % 2048, start % 2048 + 512)
        other = jnp.where(flag_ref[1] == start // 2048, near[rows, :], far[rows, :])
        rhs = jnp.concatenate([own[start : start + 512, :], other], 1)
        part = jnp.dot(lhs, rhs, preferred_element_type=jnp.float32)
        total = part if total is None else total + part
    total = total.astype(jnp.bfloat16)
    mine, theirs = total[:, :128], total[:, 128:]

    @pl.when(flag_ref[0] == 1)
    def _():
        keep_ref[...] = mine
        give_ref[...] = theirs

    @pl.when(flag_ref[0] == 0)
    def _():
        keep_ref[...] = theirs
        give_ref[...] = mine


def rotate_in(flag, tokens, own, other):
    vmem = pl.BlockSpec(memory_space=pltpu.VMEM)
    shape = jax.ShapeDtypeStruct((512, 128), jnp.bfloat16)
    return pl.pallas_call(
        rotate_in_kernel,
        out_shape=(shape, shape),
        in_specs=[pl.BlockSpec(memory_space=pltpu.SMEM)] + [vmem] * 7,
        out_specs=(vmem, vmem),
        compiler_params=pltpu.CompilerParams(vmem_limit_bytes=ROOM),
        cost_estimate=pl.CostEstimate(
            flops=2 * 512 * 256 * 4096, bytes_accessed=6_500_000, transcendentals=0
        ),
        name="rotate_in",
    )(flag, *tokens, own, *other)


def rotate_out_kernel(place_ref, *refs):
    tokens, own, windows, (own_ref, other_ref) = refs[:8], refs[8], refs[9:13], refs[13:15]
    kept_own, kept_other, kept_tokens, sems = refs[15:17], refs[17:19], refs[19:21], refs[21]
    copies = []
    for i in range(2):
        rows = [pl.multiple_of(place_ref[2 + 2 * i + j], 16) for j in range(2)]
        for start, size in CUTS:
            lanes = slice(start, start + size)
            offset = pl.multiple_of(place_ref[i] + start, 128)
            group = [(own.at[:, pl.ds(offset, size)], kept_own[i].at[:, lanes])]
            for j in range(2):
                target = kept_other[i].at[pl.ds(rows[j], 176), lanes]
                group.append((windows[2 * i + j].at[:, lanes], target))
            for half in range(2):
                for piece in range(4):
                    target = kept_tokens[i].at[
                        half * 2 : half * 2 + 2, piece * 32 : piece * 32 + 32, lanes
                    ]
                    source = tokens[half * 4 + piece].at[:, :, pl.ds(offset, size)]
                    group.append((source, target))
            copies.append(
                [
                    pltpu.make_async_copy(source, target, sems.at[11 * len(copies) + j])
                    for j, (source, target) in enumerate(group)
                ]
            )
    for group in copies:
        for copy in group:
            copy.start()
    total = [None, None]
    for i, group in enumerate(copies):
        for copy in group:
            copy.wait()
        start, size = CUTS[i % 2]
        lanes = slice(start, start + size)
        basis = jnp.concatenate([kept_other[i // 2][:, lanes], kept_own[i // 2][:, lanes]], 0)
        for half in range(2):
            part = lax.dot_general(
                basis,
                kept_tokens[i // 2][half * 2 : half * 2 + 2, :, lanes].reshape(256, size),
                (((1,), (1,)), ((), ())),
                preferred_element_type=jnp.float32,
            )
            total[half] = part if total[half] is None else total[half] + part
    swap = place_ref[6] == 0
    for half in range(2):
        lanes = slice(half * 256, half * 256 + 256)
        own_ref[:, lanes] = total[half][352:].astype(own_ref.dtype)
        low, high = total[half][:176], total[half][176:352]
        rows = jnp.concatenate([jnp.where(swap, low, high), jnp.where(swap, high, low)[8:]], 0)
        other_ref[:, lanes] = rows.astype(other_ref.dtype)


def rotate_out(places, tokens, own, windows):
    shape = jax.ShapeDtypeStruct((344, 512), jnp.bfloat16)
    anywhere = pl.BlockSpec(memory_space=pltpu.HBM)
    vmem = pl.BlockSpec(memory_space=pltpu.VMEM)
    return pl.pallas_call(
        rotate_out_kernel,
        out_shape=(shape, shape),
        in_specs=[pl.BlockSpec(memory_space=pltpu.SMEM)] + [anywhere] * 13,
        out_specs=(vmem, vmem),
        scratch_shapes=[pltpu.VMEM((344, 5504), jnp.bfloat16)] * 2
        + [pltpu.VMEM((352, 5504), jnp.bfloat16)] * 2
        + [pltpu.VMEM((4, 128, 5504), jnp.bfloat16)] * 2
        + [pltpu.SemaphoreType.DMA((44,))],
        compiler_params=pltpu.CompilerParams(vmem_limit_bytes=ROOM),
        cost_estimate=pl.CostEstimate(
            flops=2 * 512 * 696 * 11008, bytes_accessed=(512 + 696) * 22016, transcendentals=0
        ),
        name="rotate_out",
    )(places, *tokens, own, *windows)


def product_kernel(place_ref, *refs):
    lefts, rights, (keep_ref, give_ref) = refs[:4], refs[4:8], refs[8:]

    def left(half, group, example):
        lane = (half * 2 + example) * 128
        pair = [lefts[group * 2 + i] for i in range(2)]
        return jnp.concatenate([r[:, lane : lane + 128] for r in pair], 1)

    def right(half, piece, example):
        ref = rights[half * 2 + piece // 8]
        tiles = []
        for side in range(2):
            for u in range(8):
                row = side * 128 + (u ^ (piece >> 1)) * 16
                tiles.append(ref[piece % 8, example, row : row + 16, :])
        return jnp.concatenate(tiles, 0)

    for pair in range(8):
        sources = (2 * pair, 2 * pair + 1)
        total = None
        for half in range(2):
            pieces = [s if half == 0 else (s % 4) * 4 + s // 4 for s in sources]
            for group in range(2):
                for example in range(2):
                    rhs = jnp.concatenate(
                        [right(half, piece, group * 2 + example) for piece in pieces], 1
                    )
                    product = jnp.dot(
                        left(half, group, example), rhs, preferred_element_type=jnp.float32
                    )
                    square = product * product
                    total = square if total is None else total + square
        total = total * (1.0 / 16.0)
        for i, s in enumerate(sources):
            place = place_ref[s]
            column = pl.multiple_of(lax.rem(place, 8) * 128, 128)
            part = total[:, i * 128 : (i + 1) * 128]

            @pl.when(place < 8)
            def _(part=part, column=column):
                keep_ref[:, pl.ds(column, 128)] = part

            @pl.when(place >= 8)
            def _(part=part, column=column):
                give_ref[:, pl.ds(column, 128)] = part


def product(places, lefts, rights):
    rows = lefts[0].shape[0]
    shape = jax.ShapeDtypeStruct((rows, 1024), jnp.float32)
    vmem = pl.BlockSpec(memory_space=pltpu.VMEM)
    return pl.pallas_call(
        product_kernel,
        out_shape=(shape, shape),
        in_specs=[pl.BlockSpec(memory_space=pltpu.SMEM)] + [vmem] * 8,
        out_specs=(vmem, vmem),
        compiler_params=pltpu.CompilerParams(vmem_limit_bytes=24 * 1024 * 1024),
        cost_estimate=pl.CostEstimate(
            flops=2 * 8 * 256 * rows * 2048, bytes_accessed=14_000_000, transcendentals=0
        ),
        name="squares",
    )(places, *lefts, *rights)


def per_device(acts, grads, basis_in, basis_out):
    core, zl, zh = lax.axis_index("c"), lax.axis_index("zl"), lax.axis_index("zh")
    y, x = lax.axis_index("y"), lax.axis_index("x")
    steps = [steps_of(half) for half in range(2)]
    halves = range(2)

    def moved(v, step, *others):
        return [steps[half][step](after(v[half], *others) if others else v[half]) for half in halves]

    def joined(v, w, axis):
        return [jnp.concatenate([v[half], w[half]], axis) for half in halves]

    basis_out = basis_out.T

    a0 = [acts[2 * half : 2 * half + 2] for half in halves]
    g0 = [grads[2 * half : 2 * half + 2] for half in halves]
    a1 = joined(a0, moved(a0, 0), 1)
    part = flip_both(lax.dynamic_slice_in_dim(basis_in, 2048 * (1 - zl), 2048, 0))
    other_in = part, flip_zl(part)
    window = lax.dynamic_slice(basis_out, (168 * (1 - zl), 5504 * core), (176, 5504))
    g1 = joined(g0, moved(g0, 0), 1)
    a2 = joined(a1, moved(a1, 1), 1)
    first = relay(after(window, part), ("both", None))
    g2 = joined(g1, moved(g1, 1), 1)
    a3 = joined(a2, moved(a2, 2), 1)
    a4 = moved(a3, 3)

    flag = jnp.stack([(zh == zl).astype(jnp.int32), zl.astype(jnp.int32)])
    acts_pieces = [a3[0], a4[0], a3[1], a4[1]]
    keep, give = rotate_in(after(flag, first, *g2), acts_pieces, basis_in, other_in)
    keep, give = keep.reshape(4, 128, 128), give.reshape(4, 128, 128)
    exchanged = flip_zh(keep), flip_zl(give), flip_both(give)
    g3 = moved(g2, 2, *a4)
    g4 = moved(g2, 3, *exchanged)
    near = jnp.concatenate([after(keep, *g3), exchanged[0]], 1)
    far = jnp.concatenate(after(exchanged[1:], *g3), 1)

    c0 = [
        jnp.concatenate([near[2 * half : 2 * half + 2], far[2 * half : 2 * half + 2]], 0)
        for half in halves
    ]
    swapped = [v.reshape(4, 16, 2, 8, 128)[:, :, ::-1].reshape(4, 256, 128) for v in c0]
    c1 = [jnp.stack([c0[half], v]) for half, v in enumerate(moved(swapped, 0))]
    second = relay(after(jnp.where(core == 0, first, window), *exchanged), ("zl", "both"))
    third = relay(after(second, *c1, *g4), (None, "zl"))

    c2 = joined(c1, moved(c1, 1), 0)
    g5 = moved(g3, 3, *c1, *g4)
    grads_pieces = [v[half] for half in halves for v in (g2, g3, g4, g5)]
    c3 = joined(c2, moved(c2, 2), 0)
    c4 = moved(c3, 3, *g5)
    outer = jnp.where(core == 0, first, third)
    places = [5504 * core, 5504 * (1 - core)]
    places += [176 * core, 176 * (1 - core), 176 * core, 176 * (1 - core), zl]
    windows = [outer, second, flip_core(after(second, *c2)), flip_core(after(outer, *c2))]
    places = after(jnp.stack(places).astype(jnp.int32), *c3)
    mine, theirs = rotate_out(places, grads_pieces, basis_out, windows)
    rights = [v[half] for half in halves for v in (c3, c4)]
    lefts = [mine, flip_zh(theirs), flip_zl(mine), flip_both(theirs)]

    low, high = jnp.where(core == 0, 1, 3), jnp.where(core == 0, 3, 1)

    def mask(bits):
        return (low if bits & 1 else 0) ^ (high if bits & 2 else 0)

    places = jnp.stack(
        [((y ^ mask(s // 4)) * 4 + (x ^ mask(s % 4))) ^ (core * 8) for s in range(16)]
    ).astype(jnp.int32)
    keep, give = product(places, lefts, rights)
    return keep + flip_core(give)


def solution(mesh):
    fine = Mesh(mesh.devices.reshape(2, 2, 2, 4, 4), AXES)
    dp, eig = ("zl", "c"), ("zh", "y", "x")
    placed = (P(dp, eig, None), P(dp, eig, None), P(None, eig), P(None, eig))
    return jax.shard_map(
        per_device, mesh=fine, in_specs=placed, out_specs=P(eig, dp), check_vma=False
    )
```

```python
import jax
import jax.numpy as jnp
from jax import lax
from jax.experimental import pallas as pl
from jax.experimental.pallas import tpu as pltpu
from jax.sharding import Mesh
from jax.sharding import PartitionSpec as P

AXES = ("zl", "c", "zh", "y", "x")
ROOM = 54 * 1024 * 1024
CUTS = (((0, 1024), (1024, 1792), (2816, 2688)), ((0, 2688), (2688, 1792), (4480, 1024)))


def relay(v, hops):
    table = []
    for core, hop in enumerate(hops):
        for zl in range(2):
            for zh in range(2):
                to = {"both": (1 - zl, 1 - zh), "zl": (1 - zl, zh)}.get(hop)
                if to:
                    table.append((zl * 4 + core * 2 + zh, to[0] * 4 + core * 2 + to[1]))
    return lax.ppermute(v, ("zl", "c", "zh"), table)


def near_pairs(axis, step):
    masks = ((1, 3), (3, 1))
    table = [
        (core * 4 + i, core * 4 + (i ^ masks[core][step])) for core in range(2) for i in range(4)
    ]
    return lambda v: lax.ppermute(v, ("c", axis), table)


def steps_of(half):
    first, second = ("x", "y") if half == 0 else ("y", "x")
    return [near_pairs(axis, step) for axis in (first, second) for step in range(2)]


def flip_zh(v):
    return lax.ppermute(v, "zh", [(0, 1), (1, 0)])


def flip_zl(v):
    return lax.ppermute(v, "zl", [(0, 1), (1, 0)])


def flip_both(v):
    return lax.ppermute(v, ("zl", "zh"), [(i, 3 - i) for i in range(4)])


def flip_core(v):
    return lax.ppermute(v, "c", [(0, 1), (1, 0)])


def after(v, *others):
    return lax.optimization_barrier((v, *others))[0]


def rotate_in_kernel(flag_ref, *refs):
    tokens, own, (near, far), (keep_ref, give_ref) = refs[:4], refs[4], refs[5:7], refs[7:]
    total = None
    for start in range(0, 4096, 512):
        lhs = jnp.concatenate(
            [
                tokens[half * 2 + piece][example, :, start : start + 512]
                for half in range(2)
                for example in range(2)
                for piece in range(2)
            ],
            0,
        )
        rows = slice(start % 2048, start % 2048 + 512)
        other = jnp.where(flag_ref[1] == start // 2048, near[rows, :], far[rows, :])
        rhs = jnp.concatenate([own[start : start + 512, :], other], 1)
        part = jnp.dot(lhs, rhs, preferred_element_type=jnp.float32)
        total = part if total is None else total + part
    total = total.astype(jnp.bfloat16)
    mine, theirs = total[:, :128], total[:, 128:]

    @pl.when(flag_ref[0] == 1)
    def _():
        keep_ref[...] = mine
        give_ref[...] = theirs

    @pl.when(flag_ref[0] == 0)
    def _():
        keep_ref[...] = theirs
        give_ref[...] = mine


def rotate_in(flag, tokens, own, other):
    vmem = pl.BlockSpec(memory_space=pltpu.VMEM)
    shape = jax.ShapeDtypeStruct((512, 128), jnp.bfloat16)
    return pl.pallas_call(
        rotate_in_kernel,
        out_shape=(shape, shape),
        in_specs=[pl.BlockSpec(memory_space=pltpu.SMEM)] + [vmem] * 7,
        out_specs=(vmem, vmem),
        compiler_params=pltpu.CompilerParams(vmem_limit_bytes=24 * 1024 * 1024),
        cost_estimate=pl.CostEstimate(
            flops=2 * 512 * 256 * 4096, bytes_accessed=6_500_000, transcendentals=0
        ),
        name="rotate_in",
    )(flag, *tokens, own, *other)


def rotate_out_kernel(place_ref, *refs):
    tokens, own, windows, (own_ref, other_ref) = refs[:8], refs[8], refs[9:13], refs[13:15]
    kept_own, kept_other, kept_tokens, sems = refs[15:17], refs[17:19], refs[19:21], refs[21]
    copies = []
    for i in range(2):
        rows = [pl.multiple_of(place_ref[2 + 2 * i + j], 16) for j in range(2)]
        for start, size in CUTS[i]:
            lanes = slice(start, start + size)
            offset = pl.multiple_of(place_ref[i] + start, 128)
            group = [(own.at[:, pl.ds(offset, size)], kept_own[i].at[:, lanes])]
            for j in range(2):
                target = kept_other[i].at[pl.ds(rows[j], 176), lanes]
                group.append((windows[2 * i + j].at[:, lanes], target))
            for half in range(2):
                for piece in range(4):
                    target = kept_tokens[i].at[
                        half * 2 : half * 2 + 2, piece * 32 : piece * 32 + 32, lanes
                    ]
                    source = tokens[half * 4 + piece].at[:, :, pl.ds(offset, size)]
                    group.append((source, target))
            copies.append(
                (
                    i,
                    lanes,
                    [
                        pltpu.make_async_copy(source, target, sems.at[11 * len(copies) + j])
                        for j, (source, target) in enumerate(group)
                    ],
                )
            )
    for _, _, group in copies:
        for copy in group:
            copy.start()
    total = [None, None]
    for i, lanes, group in copies:
        for copy in group:
            copy.wait()
        size = lanes.stop - lanes.start
        basis = jnp.concatenate([kept_other[i][:, lanes], kept_own[i][:, lanes]], 0)
        for half in range(2):
            part = lax.dot_general(
                basis,
                kept_tokens[i][half * 2 : half * 2 + 2, :, lanes].reshape(256, size),
                (((1,), (1,)), ((), ())),
                preferred_element_type=jnp.float32,
            )
            total[half] = part if total[half] is None else total[half] + part
    swap = place_ref[6] == 0
    for half in range(2):
        lanes = slice(half * 256, half * 256 + 256)
        own_ref[:, lanes] = total[half][352:].astype(own_ref.dtype)
        low, high = total[half][:176], total[half][176:352]
        rows = jnp.concatenate([jnp.where(swap, low, high), jnp.where(swap, high, low)[8:]], 0)
        other_ref[:, lanes] = rows.astype(other_ref.dtype)


def rotate_out(places, tokens, own, windows):
    shape = jax.ShapeDtypeStruct((344, 512), jnp.bfloat16)
    anywhere = pl.BlockSpec(memory_space=pltpu.HBM)
    vmem = pl.BlockSpec(memory_space=pltpu.VMEM)
    return pl.pallas_call(
        rotate_out_kernel,
        out_shape=(shape, shape),
        in_specs=[pl.BlockSpec(memory_space=pltpu.SMEM)]
        + ([anywhere] * 3 + [vmem]) * 2
        + [anywhere] * 5,
        out_specs=(vmem, vmem),
        scratch_shapes=[pltpu.VMEM((344, 5504), jnp.bfloat16)] * 2
        + [pltpu.VMEM((352, 5504), jnp.bfloat16)] * 2
        + [pltpu.VMEM((4, 128, 5504), jnp.bfloat16)] * 2
        + [pltpu.SemaphoreType.DMA((66,))],
        compiler_params=pltpu.CompilerParams(vmem_limit_bytes=ROOM),
        cost_estimate=pl.CostEstimate(
            flops=2 * 512 * 696 * 11008, bytes_accessed=(512 + 696) * 22016, transcendentals=0
        ),
        name="rotate_out",
    )(places, *tokens, own, *windows)


def product_kernel(place_ref, *refs):
    lefts, rights, (keep_ref, give_ref) = refs[:4], refs[4:8], refs[8:]

    def left(half, group, example):
        lane = (half * 2 + example) * 128
        pair = [lefts[group * 2 + i] for i in range(2)]
        return jnp.concatenate([r[:, lane : lane + 128] for r in pair], 1)

    def right(half, piece, example):
        ref = rights[half * 2 + piece // 8]
        tiles = []
        for side in range(2):
            for u in range(8):
                row = side * 128 + (u ^ (piece >> 1)) * 16
                tiles.append(ref[piece % 8, example, row : row + 16, :])
        return jnp.concatenate(tiles, 0)

    for pair in range(8):
        sources = (2 * pair, 2 * pair + 1)
        total = None
        for half in range(2):
            pieces = [s if half == 0 else (s % 4) * 4 + s // 4 for s in sources]
            for group in range(2):
                for example in range(2):
                    rhs = jnp.concatenate(
                        [right(half, piece, group * 2 + example) for piece in pieces], 1
                    )
                    product = jnp.dot(
                        left(half, group, example), rhs, preferred_element_type=jnp.float32
                    )
                    square = product * product
                    total = square if total is None else total + square
        total = total * (1.0 / 16.0)
        for i, s in enumerate(sources):
            place = place_ref[s]
            column = pl.multiple_of(lax.rem(place, 8) * 128, 128)
            part = total[:, i * 128 : (i + 1) * 128]

            @pl.when(place < 8)
            def _(part=part, column=column):
                keep_ref[:, pl.ds(column, 128)] = part

            @pl.when(place >= 8)
            def _(part=part, column=column):
                give_ref[:, pl.ds(column, 128)] = part


def product(places, lefts, rights):
    rows = lefts[0].shape[0]
    shape = jax.ShapeDtypeStruct((rows, 1024), jnp.float32)
    vmem = pl.BlockSpec(memory_space=pltpu.VMEM)
    return pl.pallas_call(
        product_kernel,
        out_shape=(shape, shape),
        in_specs=[pl.BlockSpec(memory_space=pltpu.SMEM)] + [vmem] * 8,
        out_specs=(vmem, vmem),
        compiler_params=pltpu.CompilerParams(vmem_limit_bytes=24 * 1024 * 1024),
        cost_estimate=pl.CostEstimate(
            flops=2 * 8 * 256 * rows * 2048, bytes_accessed=14_000_000, transcendentals=0
        ),
        name="squares",
    )(places, *lefts, *rights)


def per_device(acts, grads, basis_in, basis_out):
    core, zl, zh = lax.axis_index("c"), lax.axis_index("zl"), lax.axis_index("zh")
    y, x = lax.axis_index("y"), lax.axis_index("x")
    steps = [steps_of(half) for half in range(2)]
    halves = range(2)

    def moved(v, step, *others):
        return [steps[half][step](after(v[half], *others) if others else v[half]) for half in halves]

    def joined(v, w, axis):
        return [jnp.concatenate([v[half], w[half]], axis) for half in halves]

    basis_out = basis_out.T

    g0 = [grads[2 * half : 2 * half + 2] for half in halves]
    a0 = [acts[2 * half : 2 * half + 2] for half in halves]
    a1 = joined(a0, moved(a0, 0), 1)
    part = flip_both(lax.dynamic_slice_in_dim(basis_in, 2048 * (1 - zl), 2048, 0))
    other_in = part, flip_zl(part)
    window = lax.dynamic_slice(basis_out, (168 * (1 - zl), 5504 * core), (176, 5504))
    g1 = joined(g0, moved(g0, 0), 1)
    a2 = joined(a1, moved(a1, 1), 1)
    first = relay(after(window, part), ("both", None))
    g2 = joined(g1, moved(g1, 1), 1)
    a3 = joined(a2, moved(a2, 2), 1)
    a4 = moved(a3, 3)

    flag = jnp.stack([(zh == zl).astype(jnp.int32), zl.astype(jnp.int32)])
    acts_pieces = [a3[0], a4[0], a3[1], a4[1]]
    keep, give = rotate_in(after(flag, first, *g2), acts_pieces, basis_in, other_in)
    keep, give = keep.reshape(4, 128, 128), give.reshape(4, 128, 128)
    exchanged = flip_zh(keep), flip_zl(give), flip_both(give)
    g3 = moved(g2, 2, *a4)
    g4 = moved(g2, 3, keep)
    near = jnp.concatenate([after(keep, *g3), exchanged[0]], 1)
    far = jnp.concatenate(after(exchanged[1:], *g3), 1)

    c0 = [
        jnp.concatenate([near[2 * half : 2 * half + 2], far[2 * half : 2 * half + 2]], 0)
        for half in halves
    ]
    swapped = [v.reshape(4, 16, 2, 8, 128)[:, :, ::-1].reshape(4, 256, 128) for v in c0]
    c1 = [jnp.stack([c0[half], v]) for half, v in enumerate(moved(swapped, 0))]
    second = relay(after(jnp.where(core == 0, first, window), *exchanged), ("zl", "both"))
    third = relay(after(second, *c1, *g4), (None, "zl"))

    c2 = joined(c1, moved(c1, 1), 0)
    g5 = moved(g3, 3, *g4)
    grads_pieces = [v[half] for half in halves for v in (g2, g3, g4, g5)]
    c3 = joined(c2, moved(c2, 2), 0)
    c4 = moved(c3, 3, *g5)
    outer = jnp.where(core == 0, first, third)
    places = [5504 * core, 5504 * (1 - core)]
    places += [176 * core, 176 * (1 - core), 176 * core, 176 * (1 - core), zl]
    windows = [outer, second, flip_core(after(second, *c2)), flip_core(after(outer, *c2))]
    places = after(jnp.stack(places).astype(jnp.int32), *c3)
    mine, theirs = rotate_out(places, grads_pieces, basis_out, windows)
    rights = [v[half] for half in halves for v in (c3, c4)]
    lefts = [mine, flip_zh(theirs), flip_zl(mine), flip_both(theirs)]

    low, high = jnp.where(core == 0, 1, 3), jnp.where(core == 0, 3, 1)

    def mask(bits):
        return (low if bits & 1 else 0) ^ (high if bits & 2 else 0)

    places = jnp.stack(
        [((y ^ mask(s // 4)) * 4 + (x ^ mask(s % 4))) ^ (core * 8) for s in range(16)]
    ).astype(jnp.int32)
    keep, give = product(places, lefts, rights)
    return keep + flip_core(give)


def solution(mesh):
    fine = Mesh(mesh.devices.reshape(2, 2, 2, 4, 4), AXES)
    dp, eig = ("zl", "c"), ("zh", "y", "x")
    placed = (P(dp, eig, None), P(dp, eig, None), P(None, eig), P(None, eig))
    return jax.shard_map(
        per_device, mesh=fine, in_specs=placed, out_specs=P(eig, dp), check_vma=False
    )
```

```python
import jax
import jax.numpy as jnp
from jax import lax
from jax.experimental import pallas as pl
from jax.experimental.pallas import tpu as pltpu
from jax.sharding import Mesh
from jax.sharding import PartitionSpec as P

AXES = ("zl", "c", "zh", "y", "x")
ROOM = 54 * 1024 * 1024
CUTS = (((0, 1024), (1024, 1792), (2816, 2688)), ((0, 2688), (2688, 1792), (4480, 1024)))


def relay(v, hops):
    table = []
    for core, hop in enumerate(hops):
        for zl in range(2):
            for zh in range(2):
                to = {"both": (1 - zl, 1 - zh), "zl": (1 - zl, zh)}.get(hop)
                if to:
                    table.append((zl * 4 + core * 2 + zh, to[0] * 4 + core * 2 + to[1]))
    return lax.ppermute(v, ("zl", "c", "zh"), table)


def near_pairs(axis, step):
    masks = ((1, 3), (3, 1))
    table = [
        (core * 4 + i, core * 4 + (i ^ masks[core][step])) for core in range(2) for i in range(4)
    ]
    return lambda v: lax.ppermute(v, ("c", axis), table)


def steps_of(half):
    first, second = ("x", "y") if half == 0 else ("y", "x")
    return [near_pairs(axis, step) for axis in (first, second) for step in range(2)]


def flip_zh(v):
    return lax.ppermute(v, "zh", [(0, 1), (1, 0)])


def flip_zl(v):
    return lax.ppermute(v, "zl", [(0, 1), (1, 0)])


def flip_both(v):
    return lax.ppermute(v, ("zl", "zh"), [(i, 3 - i) for i in range(4)])


def flip_core(v):
    return lax.ppermute(v, "c", [(0, 1), (1, 0)])


def after(v, *others):
    return lax.optimization_barrier((v, *others))[0]


def rotate_in_kernel(flag_ref, *refs):
    tokens, own, (near, far), (keep_ref, give_ref) = refs[:4], refs[4], refs[5:7], refs[7:]
    total = None
    for start in range(0, 4096, 512):
        lhs = jnp.concatenate(
            [
                tokens[half * 2 + piece][example, :, start : start + 512]
                for half in range(2)
                for example in range(2)
                for piece in range(2)
            ],
            0,
        )
        rows = slice(start % 2048, start % 2048 + 512)
        other = jnp.where(flag_ref[1] == start // 2048, near[rows, :], far[rows, :])
        rhs = jnp.concatenate([own[start : start + 512, :], other], 1)
        part = jnp.dot(lhs, rhs, preferred_element_type=jnp.float32)
        total = part if total is None else total + part
    total = total.astype(jnp.bfloat16)
    mine, theirs = total[:, :128], total[:, 128:]

    @pl.when(flag_ref[0] == 1)
    def _():
        keep_ref[...] = mine
        give_ref[...] = theirs

    @pl.when(flag_ref[0] == 0)
    def _():
        keep_ref[...] = theirs
        give_ref[...] = mine


def rotate_in(flag, tokens, own, other):
    vmem = pl.BlockSpec(memory_space=pltpu.VMEM)
    shape = jax.ShapeDtypeStruct((512, 128), jnp.bfloat16)
    return pl.pallas_call(
        rotate_in_kernel,
        out_shape=(shape, shape),
        in_specs=[pl.BlockSpec(memory_space=pltpu.SMEM)] + [vmem] * 7,
        out_specs=(vmem, vmem),
        compiler_params=pltpu.CompilerParams(vmem_limit_bytes=24 * 1024 * 1024),
        cost_estimate=pl.CostEstimate(
            flops=2 * 512 * 256 * 4096, bytes_accessed=6_500_000, transcendentals=0
        ),
        name="rotate_in",
    )(flag, *tokens, own, *other)


def rotate_out_kernel(place_ref, *refs):
    tokens, own, windows, (own_ref, other_ref) = refs[:8], refs[8], refs[9:13], refs[13:15]
    kept_own, kept_other, kept_tokens, sems = refs[15:17], refs[17:19], refs[19:21], refs[21]
    copies = []
    for i in range(2):
        rows = [pl.multiple_of(place_ref[2 + 2 * i + j], 16) for j in range(2)]
        for start, size in CUTS[i]:
            lanes = slice(start, start + size)
            offset = pl.multiple_of(place_ref[i] + start, 128)
            group = [(own.at[:, pl.ds(offset, size)], kept_own[i].at[:, lanes])]
            for j in range(2):
                target = kept_other[i].at[pl.ds(rows[j], 176), lanes]
                group.append((windows[2 * i + j].at[:, lanes], target))
            for half in range(2):
                for piece in range(4):
                    target = kept_tokens[i].at[
                        half * 2 : half * 2 + 2, piece * 32 : piece * 32 + 32, lanes
                    ]
                    source = tokens[half * 4 + piece].at[:, :, pl.ds(offset, size)]
                    group.append((source, target))
            copies.append(
                (
                    i,
                    lanes,
                    [
                        pltpu.make_async_copy(source, target, sems.at[11 * len(copies) + j])
                        for j, (source, target) in enumerate(group)
                    ],
                )
            )
    for _, _, group in copies:
        for copy in group:
            copy.start()
    total = [None, None]
    for i, lanes, group in copies:
        for copy in group:
            copy.wait()
        size = lanes.stop - lanes.start
        basis = jnp.concatenate([kept_other[i][:, lanes], kept_own[i][:, lanes]], 0)
        for half in range(2):
            part = lax.dot_general(
                basis,
                kept_tokens[i][half * 2 : half * 2 + 2, :, lanes].reshape(256, size),
                (((1,), (1,)), ((), ())),
                preferred_element_type=jnp.float32,
            )
            total[half] = part if total[half] is None else total[half] + part
    swap = place_ref[6] == 0
    for half in range(2):
        lanes = slice(half * 256, half * 256 + 256)
        own_ref[:, lanes] = total[half][352:].astype(own_ref.dtype)
        low, high = total[half][:176], total[half][176:352]
        rows = jnp.concatenate([jnp.where(swap, low, high), jnp.where(swap, high, low)[8:]], 0)
        other_ref[:, lanes] = rows.astype(other_ref.dtype)


def rotate_out(places, tokens, own, windows):
    shape = jax.ShapeDtypeStruct((344, 512), jnp.bfloat16)
    anywhere = pl.BlockSpec(memory_space=pltpu.HBM)
    vmem = pl.BlockSpec(memory_space=pltpu.VMEM)
    return pl.pallas_call(
        rotate_out_kernel,
        out_shape=(shape, shape),
        in_specs=[pl.BlockSpec(memory_space=pltpu.SMEM)]
        + ([anywhere] * 3 + [vmem]) * 2
        + [anywhere] * 5,
        out_specs=(vmem, vmem),
        scratch_shapes=[pltpu.VMEM((344, 5504), jnp.bfloat16)] * 2
        + [pltpu.VMEM((352, 5504), jnp.bfloat16)] * 2
        + [pltpu.VMEM((4, 128, 5504), jnp.bfloat16)] * 2
        + [pltpu.SemaphoreType.DMA((66,))],
        compiler_params=pltpu.CompilerParams(vmem_limit_bytes=ROOM),
        cost_estimate=pl.CostEstimate(
            flops=2 * 512 * 696 * 11008, bytes_accessed=(512 + 696) * 22016, transcendentals=0
        ),
        name="rotate_out",
    )(places, *tokens, own, *windows)


def product_kernel(place_ref, *refs):
    lefts, sources, (keep_ref, give_ref) = refs[:4], refs[4:8], refs[8:10]
    rights, sems = refs[10:14], refs[14]
    copies = [pltpu.make_async_copy(sources[i], rights[i], sems.at[i]) for i in range(4)]
    for i in (0, 2, 1, 3):
        copies[i].start()

    def left(half, group, example):
        lane = (half * 2 + example) * 128
        pair = [lefts[group * 2 + i] for i in range(2)]
        return jnp.concatenate([r[:, lane : lane + 128] for r in pair], 1)

    def right(half, piece, example):
        ref = rights[half * 2 + piece // 8]
        tiles = []
        for side in range(2):
            for u in range(8):
                row = side * 128 + (u ^ (piece >> 1)) * 16
                tiles.append(ref[piece % 8, example, row : row + 16, :])
        return jnp.concatenate(tiles, 0)

    for first, arrived in ((0, (0, 2)), (8, (1,)), (2, (3,)), (10, ())):
        for i in arrived:
            copies[i].wait()
        blocks = (first, first + 1, first + 4, first + 5)
        total = None
        for half in range(2):
            pieces = [s if half == 0 else (s % 4) * 4 + s // 4 for s in blocks]
            for group in range(2):
                for example in range(2):
                    rhs = jnp.concatenate(
                        [right(half, piece, group * 2 + example) for piece in pieces], 1
                    )
                    product = jnp.dot(
                        left(half, group, example), rhs, preferred_element_type=jnp.float32
                    )
                    square = product * product
                    total = square if total is None else total + square
        total = total * (1.0 / 16.0)
        for i, s in enumerate(blocks):
            place = place_ref[s]
            column = pl.multiple_of(lax.rem(place, 8) * 128, 128)
            part = total[:, i * 128 : (i + 1) * 128]

            @pl.when(place < 8)
            def _(part=part, column=column):
                keep_ref[:, pl.ds(column, 128)] = part

            @pl.when(place >= 8)
            def _(part=part, column=column):
                give_ref[:, pl.ds(column, 128)] = part


def product(places, lefts, rights):
    rows = lefts[0].shape[0]
    shape = jax.ShapeDtypeStruct((rows, 1024), jnp.float32)
    vmem = pl.BlockSpec(memory_space=pltpu.VMEM)
    return pl.pallas_call(
        product_kernel,
        out_shape=(shape, shape),
        in_specs=[pl.BlockSpec(memory_space=pltpu.SMEM)] + [vmem] * 4 + [pl.BlockSpec(memory_space=pl.ANY)] * 4,
        out_specs=(vmem, vmem),
        scratch_shapes=[pltpu.VMEM(rights[0].shape, jnp.bfloat16)] * 4
        + [pltpu.SemaphoreType.DMA((4,))],
        compiler_params=pltpu.CompilerParams(vmem_limit_bytes=24 * 1024 * 1024),
        cost_estimate=pl.CostEstimate(
            flops=2 * 8 * 256 * rows * 2048, bytes_accessed=14_000_000, transcendentals=0
        ),
        name="squares",
    )(places, *lefts, *rights)


def per_device(acts, grads, basis_in, basis_out):
    core, zl, zh = lax.axis_index("c"), lax.axis_index("zl"), lax.axis_index("zh")
    y, x = lax.axis_index("y"), lax.axis_index("x")
    steps = [steps_of(half) for half in range(2)]
    halves = range(2)

    def moved(v, step, *others):
        return [steps[half][step](after(v[half], *others) if others else v[half]) for half in halves]

    def joined(v, w, axis):
        return [jnp.concatenate([v[half], w[half]], axis) for half in halves]

    basis_out = basis_out.T

    g0 = [grads[2 * half : 2 * half + 2] for half in halves]
    a0 = [acts[2 * half : 2 * half + 2] for half in halves]
    a1 = joined(a0, moved(a0, 0), 1)
    part = flip_both(lax.dynamic_slice_in_dim(basis_in, 2048 * (1 - zl), 2048, 0))
    other_in = part, flip_zl(part)
    window = lax.dynamic_slice(basis_out, (168 * (1 - zl), 5504 * core), (176, 5504))
    g1 = joined(g0, moved(g0, 0), 1)
    a2 = joined(a1, moved(a1, 1), 1)
    first = relay(after(window, part), ("both", None))
    g2 = joined(g1, moved(g1, 1), 1)
    a3 = joined(a2, moved(a2, 2), 1)
    a4 = moved(a3, 3)

    flag = jnp.stack([(zh == zl).astype(jnp.int32), zl.astype(jnp.int32)])
    acts_pieces = [a3[0], a4[0], a3[1], a4[1]]
    keep, give = rotate_in(after(flag, first, *g2), acts_pieces, basis_in, other_in)
    keep, give = keep.reshape(4, 128, 128), give.reshape(4, 128, 128)
    exchanged = flip_zh(keep), flip_zl(give), flip_both(give)
    g3 = moved(g2, 2, *a4)
    g4 = moved(g2, 3, keep)
    near = jnp.concatenate([after(keep, *g3), exchanged[0]], 1)
    far = jnp.concatenate(after(exchanged[1:], *g3), 1)

    c0 = [
        jnp.concatenate([near[2 * half : 2 * half + 2], far[2 * half : 2 * half + 2]], 0)
        for half in halves
    ]
    swapped = [v.reshape(4, 16, 2, 8, 128)[:, :, ::-1].reshape(4, 256, 128) for v in c0]
    c1 = [jnp.stack([c0[half], v]) for half, v in enumerate(moved(swapped, 0))]
    second = relay(after(jnp.where(core == 0, first, window), *exchanged), ("zl", "both"))
    third = relay(after(second, *c1, *g4), (None, "zl"))

    c2 = joined(c1, moved(c1, 1), 0)
    g5 = moved(g3, 3, *g4)
    grads_pieces = [v[half] for half in halves for v in (g2, g3, g4, g5)]
    c3 = joined(c2, moved(c2, 2), 0)
    c4 = moved(c3, 3, *g5)
    outer = jnp.where(core == 0, first, third)
    places = [5504 * core, 5504 * (1 - core)]
    places += [176 * core, 176 * (1 - core), 176 * core, 176 * (1 - core), zl]
    windows = [outer, second, flip_core(after(second, *c2)), flip_core(after(outer, *c2))]
    places = after(jnp.stack(places).astype(jnp.int32), *c3)
    mine, theirs = rotate_out(places, grads_pieces, basis_out, windows)
    rights = [v[half] for half in halves for v in (c3, c4)]
    lefts = [mine, flip_zh(theirs), flip_zl(mine), flip_both(theirs)]

    low, high = jnp.where(core == 0, 1, 3), jnp.where(core == 0, 3, 1)

    def mask(bits):
        return (low if bits & 1 else 0) ^ (high if bits & 2 else 0)

    places = jnp.stack(
        [((y ^ mask(s // 4)) * 4 + (x ^ mask(s % 4))) ^ (core * 8) for s in range(16)]
    ).astype(jnp.int32)
    keep, give = product(places, lefts, rights)
    return keep + flip_core(give)


def solution(mesh):
    fine = Mesh(mesh.devices.reshape(2, 2, 2, 4, 4), AXES)
    dp, eig = ("zl", "c"), ("zh", "y", "x")
    placed = (P(dp, eig, None), P(dp, eig, None), P(None, eig), P(None, eig))
    return jax.shard_map(
        per_device, mesh=fine, in_specs=placed, out_specs=P(eig, dp), check_vma=False
    )
```

```python
import jax
import jax.numpy as jnp
from jax import lax
from jax.experimental import pallas as pl
from jax.experimental.pallas import tpu as pltpu
from jax.sharding import Mesh
from jax.sharding import PartitionSpec as P

AXES = ("zl", "c", "zh", "y", "x")
ROOM = 54 * 1024 * 1024
CUTS = (((0, 1024), (1024, 1792), (2816, 2688)), ((0, 2688), (2688, 1792), (4480, 1024)))


def relay(v, hops):
    table = []
    for core, hop in enumerate(hops):
        for zl in range(2):
            for zh in range(2):
                to = {"both": (1 - zl, 1 - zh), "zl": (1 - zl, zh)}.get(hop)
                if to:
                    table.append((zl * 4 + core * 2 + zh, to[0] * 4 + core * 2 + to[1]))
    return lax.ppermute(v, ("zl", "c", "zh"), table)


def near_pairs(axis, step):
    masks = ((1, 3), (3, 1))
    table = [
        (core * 4 + i, core * 4 + (i ^ masks[core][step])) for core in range(2) for i in range(4)
    ]
    return lambda v: lax.ppermute(v, ("c", axis), table)


def steps_of(half):
    first, second = ("x", "y") if half == 0 else ("y", "x")
    return [near_pairs(axis, step) for axis in (first, second) for step in range(2)]


def flip_zh(v):
    return lax.ppermute(v, "zh", [(0, 1), (1, 0)])


def flip_zl(v):
    return lax.ppermute(v, "zl", [(0, 1), (1, 0)])


def flip_both(v):
    return lax.ppermute(v, ("zl", "zh"), [(i, 3 - i) for i in range(4)])


def flip_core(v):
    return lax.ppermute(v, "c", [(0, 1), (1, 0)])


def after(v, *others):
    return lax.optimization_barrier((v, *others))[0]


def rotate_in_kernel(flag_ref, *refs):
    tokens, own, (near, far), (keep_ref, give_ref) = refs[:4], refs[4], refs[5:7], refs[7:]
    total = None
    for start in range(0, 4096, 512):
        lhs = jnp.concatenate(
            [
                tokens[half * 2 + piece][example, :, start : start + 512]
                for half in range(2)
                for example in range(2)
                for piece in range(2)
            ],
            0,
        )
        rows = slice(start % 2048, start % 2048 + 512)
        other = jnp.where(flag_ref[1] == start // 2048, near[rows, :], far[rows, :])
        rhs = jnp.concatenate([own[start : start + 512, :], other], 1)
        part = jnp.dot(lhs, rhs, preferred_element_type=jnp.float32)
        total = part if total is None else total + part
    total = total.astype(jnp.bfloat16)
    mine, theirs = total[:, :128], total[:, 128:]

    @pl.when(flag_ref[0] == 1)
    def _():
        keep_ref[...] = mine
        give_ref[...] = theirs

    @pl.when(flag_ref[0] == 0)
    def _():
        keep_ref[...] = theirs
        give_ref[...] = mine


def rotate_in(flag, tokens, own, other):
    vmem = pl.BlockSpec(memory_space=pltpu.VMEM)
    shape = jax.ShapeDtypeStruct((512, 128), jnp.bfloat16)
    return pl.pallas_call(
        rotate_in_kernel,
        out_shape=(shape, shape),
        in_specs=[pl.BlockSpec(memory_space=pltpu.SMEM)] + [vmem] * 7,
        out_specs=(vmem, vmem),
        compiler_params=pltpu.CompilerParams(vmem_limit_bytes=24 * 1024 * 1024),
        cost_estimate=pl.CostEstimate(
            flops=2 * 512 * 256 * 4096, bytes_accessed=6_500_000, transcendentals=0
        ),
        name="rotate_in",
    )(flag, *tokens, own, *other)


def rotate_out_kernel(place_ref, *refs):
    tokens, own, windows, (own_ref, other_ref) = refs[:8], refs[8], refs[9:13], refs[13:15]
    kept_own, kept_other, kept_tokens, sems = refs[15:17], refs[17:19], refs[19:21], refs[21]
    copies = []
    for i in range(2):
        rows = [pl.multiple_of(place_ref[2 + 2 * i + j], 16) for j in range(2)]
        for start, size in CUTS[i]:
            lanes = slice(start, start + size)
            offset = pl.multiple_of(place_ref[i] + start, 128)
            group = [(own.at[:, pl.ds(offset, size)], kept_own[i].at[:, lanes])]
            for j in range(2):
                target = kept_other[i].at[pl.ds(rows[j], 176), lanes]
                group.append((windows[2 * i + j].at[:, lanes], target))
            for half in range(2):
                for piece in range(4):
                    target = kept_tokens[i].at[
                        half * 2 : half * 2 + 2, piece * 32 : piece * 32 + 32, lanes
                    ]
                    source = tokens[half * 4 + piece].at[:, :, pl.ds(offset, size)]
                    group.append((source, target))
            copies.append(
                (
                    i,
                    lanes,
                    [
                        pltpu.make_async_copy(source, target, sems.at[11 * len(copies) + j])
                        for j, (source, target) in enumerate(group)
                    ],
                )
            )
    for _, _, group in copies:
        for copy in group:
            copy.start()
    total = [None, None]
    for i, lanes, group in copies:
        for copy in group:
            copy.wait()
        size = lanes.stop - lanes.start
        basis = jnp.concatenate([kept_other[i][:, lanes], kept_own[i][:, lanes]], 0)
        for half in range(2):
            part = lax.dot_general(
                basis,
                kept_tokens[i][half * 2 : half * 2 + 2, :, lanes].reshape(256, size),
                (((1,), (1,)), ((), ())),
                preferred_element_type=jnp.float32,
            )
            total[half] = part if total[half] is None else total[half] + part
    swap = place_ref[6] == 0
    for half in range(2):
        lanes = slice(half * 256, half * 256 + 256)
        own_ref[:, lanes] = total[half][352:].astype(own_ref.dtype)
        low, high = total[half][:176], total[half][176:352]
        rows = jnp.concatenate([jnp.where(swap, low, high), jnp.where(swap, high, low)[8:]], 0)
        other_ref[:, lanes] = rows.astype(other_ref.dtype)


def rotate_out(places, tokens, own, windows):
    shape = jax.ShapeDtypeStruct((344, 512), jnp.bfloat16)
    anywhere = pl.BlockSpec(memory_space=pltpu.HBM)
    vmem = pl.BlockSpec(memory_space=pltpu.VMEM)
    return pl.pallas_call(
        rotate_out_kernel,
        out_shape=(shape, shape),
        in_specs=[pl.BlockSpec(memory_space=pltpu.SMEM)]
        + ([anywhere] * 3 + [vmem]) * 2
        + [anywhere] * 5,
        out_specs=(vmem, vmem),
        scratch_shapes=[pltpu.VMEM((344, 5504), jnp.bfloat16)] * 2
        + [pltpu.VMEM((352, 5504), jnp.bfloat16)] * 2
        + [pltpu.VMEM((4, 128, 5504), jnp.bfloat16)] * 2
        + [pltpu.SemaphoreType.DMA((66,))],
        compiler_params=pltpu.CompilerParams(vmem_limit_bytes=ROOM),
        cost_estimate=pl.CostEstimate(
            flops=2 * 512 * 696 * 11008, bytes_accessed=(512 + 696) * 22016, transcendentals=0
        ),
        name="rotate_out",
    )(places, *tokens, own, *windows)


def product_kernel(place_ref, *refs):
    lefts, sources, (keep_ref, give_ref) = refs[:4], refs[4:8], refs[8:10]
    rights, sems = refs[10:14], refs[14]
    copies = [pltpu.make_async_copy(sources[i], rights[i], sems.at[i]) for i in range(4)]
    for i in (0, 2, 1, 3):
        copies[i].start()

    def left(half, group, example):
        lane = (half * 2 + example) * 128
        pair = [lefts[group * 2 + i] for i in range(2)]
        return jnp.concatenate([r[:, lane : lane + 128] for r in pair], 1)

    def right(half, piece, example):
        ref = rights[half * 2 + piece // 8]
        tiles = []
        for side in range(2):
            for u in range(8):
                row = side * 128 + (u ^ (piece >> 1)) * 16
                tiles.append(ref[piece % 8, example, row : row + 16, :])
        return jnp.concatenate(tiles, 0)

    for first, arrived in ((0, (0, 2)), (8, (1,)), (2, (3,)), (10, ())):
        for i in arrived:
            copies[i].wait()
        blocks = (first, first + 1, first + 4, first + 5)
        total = None
        for half in range(2):
            pieces = [s if half == 0 else (s % 4) * 4 + s // 4 for s in blocks]
            for group in range(2):
                for example in range(2):
                    rhs = jnp.concatenate(
                        [right(half, piece, group * 2 + example) for piece in pieces], 1
                    )
                    product = jnp.dot(
                        left(half, group, example), rhs, preferred_element_type=jnp.float32
                    )
                    square = product * product
                    total = square if total is None else total + square
        total = total * (1.0 / 16.0)
        for i, s in enumerate(blocks):
            place = place_ref[s]
            column = pl.multiple_of(lax.rem(place, 8) * 128, 128)
            part = total[:, i * 128 : (i + 1) * 128]

            @pl.when(place < 8)
            def _(part=part, column=column):
                keep_ref[:, pl.ds(column, 128)] = part

            @pl.when(place >= 8)
            def _(part=part, column=column):
                give_ref[:, pl.ds(column, 128)] = part


def product(places, lefts, rights):
    rows = lefts[0].shape[0]
    shape = jax.ShapeDtypeStruct((rows, 1024), jnp.float32)
    vmem = pl.BlockSpec(memory_space=pltpu.VMEM)
    return pl.pallas_call(
        product_kernel,
        out_shape=(shape, shape),
        in_specs=[pl.BlockSpec(memory_space=pltpu.SMEM)] + [vmem] * 4 + [pl.BlockSpec(memory_space=pl.ANY)] * 4,
        out_specs=(vmem, vmem),
        scratch_shapes=[pltpu.VMEM(rights[0].shape, jnp.bfloat16)] * 4
        + [pltpu.SemaphoreType.DMA((4,))],
        compiler_params=pltpu.CompilerParams(vmem_limit_bytes=24 * 1024 * 1024),
        cost_estimate=pl.CostEstimate(
            flops=2 * 8 * 256 * rows * 2048, bytes_accessed=14_000_000, transcendentals=0
        ),
        name="squares",
    )(places, *lefts, *rights)


def per_device(acts, grads, basis_in, basis_out):
    core, zl, zh = lax.axis_index("c"), lax.axis_index("zl"), lax.axis_index("zh")
    y, x = lax.axis_index("y"), lax.axis_index("x")
    steps = [steps_of(half) for half in range(2)]
    halves = range(2)

    def moved(v, step, *others):
        return [steps[half][step](after(v[half], *others) if others else v[half]) for half in halves]

    def joined(v, w, axis):
        return [jnp.concatenate([v[half], w[half]], axis) for half in halves]

    basis_out = basis_out.T

    g0 = [grads[2 * half : 2 * half + 2] for half in halves]
    a0 = [acts[2 * half : 2 * half + 2] for half in halves]
    a1 = joined(a0, moved(a0, 0), 1)
    part = flip_both(lax.dynamic_slice_in_dim(basis_in, 2048 * (1 - zl), 2048, 0))
    other_in = part, flip_zl(part)
    window = lax.dynamic_slice(basis_out, (168 * (1 - zl), 5504 * core), (176, 5504))
    g1 = joined(g0, moved(g0, 0), 1)
    a2 = joined(a1, moved(a1, 1), 1)
    first = relay(after(window, part), ("both", None))
    g2 = joined(g1, moved(g1, 1), 1)
    a3 = joined(a2, moved(a2, 2), 1)
    a4 = moved(a3, 3)

    flag = jnp.stack([(zh == zl).astype(jnp.int32), zl.astype(jnp.int32)])
    acts_pieces = [a3[0], a4[0], a3[1], a4[1]]
    keep, give = rotate_in(after(flag, first, *g2), acts_pieces, basis_in, other_in)
    keep, give = keep.reshape(4, 128, 128), give.reshape(4, 128, 128)
    exchanged = flip_zh(keep), flip_zl(give), flip_both(give)
    g3 = moved(g2, 2, a4[0])
    g4 = moved(g2, 3)
    near = jnp.concatenate([after(keep, *g3), exchanged[0]], 1)
    far = jnp.concatenate(after(exchanged[1:], *g3), 1)

    c0 = [
        jnp.concatenate([near[2 * half : 2 * half + 2], far[2 * half : 2 * half + 2]], 0)
        for half in halves
    ]
    swapped = [v.reshape(4, 16, 2, 8, 128)[:, :, ::-1].reshape(4, 256, 128) for v in c0]
    c1 = [jnp.stack([c0[half], v]) for half, v in enumerate(moved(swapped, 0))]
    second = relay(after(jnp.where(core == 0, first, window), *exchanged), ("zl", "both"))
    third = relay(after(second, *c1, *g4), (None, "zl"))

    c2 = joined(c1, moved(c1, 1), 0)
    g5 = moved(g3, 3, *g4)
    grads_pieces = [v[half] for half in halves for v in (g2, g3, g4, g5)]
    c3 = joined(c2, moved(c2, 2), 0)
    c4 = moved(c3, 3, *g5)
    outer = jnp.where(core == 0, first, third)
    places = [5504 * core, 5504 * (1 - core)]
    places += [176 * core, 176 * (1 - core), 176 * core, 176 * (1 - core), zl]
    windows = [outer, second, flip_core(after(second, *c2)), flip_core(after(outer, *c2))]
    places = after(jnp.stack(places).astype(jnp.int32), *c3)
    mine, theirs = rotate_out(places, grads_pieces, basis_out, windows)
    rights = [v[half] for half in halves for v in (c3, c4)]
    lefts = [mine, flip_zh(theirs), flip_zl(mine), flip_both(theirs)]

    low, high = jnp.where(core == 0, 1, 3), jnp.where(core == 0, 3, 1)

    def mask(bits):
        return (low if bits & 1 else 0) ^ (high if bits & 2 else 0)

    places = jnp.stack(
        [((y ^ mask(s // 4)) * 4 + (x ^ mask(s % 4))) ^ (core * 8) for s in range(16)]
    ).astype(jnp.int32)
    keep, give = product(places, lefts, rights)
    return keep + flip_core(give)


def solution(mesh):
    fine = Mesh(mesh.devices.reshape(2, 2, 2, 4, 4), AXES)
    dp, eig = ("zl", "c"), ("zh", "y", "x")
    placed = (P(dp, eig, None), P(dp, eig, None), P(None, eig), P(None, eig))
    return jax.shard_map(
        per_device, mesh=fine, in_specs=placed, out_specs=P(eig, dp), check_vma=False
    )
```

```python
import jax
import jax.numpy as jnp
from jax import lax
from jax.experimental import pallas as pl
from jax.experimental.pallas import tpu as pltpu
from jax.sharding import Mesh
from jax.sharding import PartitionSpec as P

AXES = ("zl", "c", "zh", "y", "x")
ROOM = 54 * 1024 * 1024
CUTS = (((0, 1024), (1024, 1792), (2816, 2688)), ((0, 2688), (2688, 1792), (4480, 1024)))


def relay(v, hops):
    table = []
    for core, hop in enumerate(hops):
        for zl in range(2):
            for zh in range(2):
                to = {"both": (1 - zl, 1 - zh), "zl": (1 - zl, zh)}.get(hop)
                if to:
                    table.append((zl * 4 + core * 2 + zh, to[0] * 4 + core * 2 + to[1]))
    return lax.ppermute(v, ("zl", "c", "zh"), table)


def near_pairs(axis, step):
    masks = ((1, 3), (3, 1))
    table = [
        (core * 4 + i, core * 4 + (i ^ masks[core][step])) for core in range(2) for i in range(4)
    ]
    return lambda v: lax.ppermute(v, ("c", axis), table)


def steps_of(half):
    first, second = ("x", "y") if half == 0 else ("y", "x")
    return [near_pairs(axis, step) for axis in (first, second) for step in range(2)]


def flip_zh(v):
    return lax.ppermute(v, "zh", [(0, 1), (1, 0)])


def flip_zl(v):
    return lax.ppermute(v, "zl", [(0, 1), (1, 0)])


def flip_both(v):
    return lax.ppermute(v, ("zl", "zh"), [(i, 3 - i) for i in range(4)])


def flip_core(v):
    return lax.ppermute(v, "c", [(0, 1), (1, 0)])


def after(v, *others):
    return lax.optimization_barrier((v, *others))[0]


def rotate_in_kernel(flag_ref, *refs):
    tokens, own, (near, far), (keep_ref, give_ref) = refs[:4], refs[4], refs[5:7], refs[7:]
    total = None
    for start in range(0, 4096, 512):
        lhs = jnp.concatenate(
            [
                tokens[half * 2 + piece][example, :, start : start + 512]
                for half in range(2)
                for example in range(2)
                for piece in range(2)
            ],
            0,
        )
        rows = slice(start % 2048, start % 2048 + 512)
        other = jnp.where(flag_ref[1] == start // 2048, near[rows, :], far[rows, :])
        rhs = jnp.concatenate([own[start : start + 512, :], other], 1)
        part = jnp.dot(lhs, rhs, preferred_element_type=jnp.float32)
        total = part if total is None else total + part
    total = total.astype(jnp.bfloat16)
    mine, theirs = total[:, :128], total[:, 128:]

    @pl.when(flag_ref[0] == 1)
    def _():
        keep_ref[...] = mine
        give_ref[...] = theirs

    @pl.when(flag_ref[0] == 0)
    def _():
        keep_ref[...] = theirs
        give_ref[...] = mine


def rotate_in(flag, tokens, own, other):
    vmem = pl.BlockSpec(memory_space=pltpu.VMEM)
    shape = jax.ShapeDtypeStruct((512, 128), jnp.bfloat16)
    return pl.pallas_call(
        rotate_in_kernel,
        out_shape=(shape, shape),
        in_specs=[pl.BlockSpec(memory_space=pltpu.SMEM)] + [vmem] * 7,
        out_specs=(vmem, vmem),
        compiler_params=pltpu.CompilerParams(vmem_limit_bytes=24 * 1024 * 1024),
        cost_estimate=pl.CostEstimate(
            flops=2 * 512 * 256 * 4096, bytes_accessed=6_500_000, transcendentals=0
        ),
        name="rotate_in",
    )(flag, *tokens, own, *other)


def rotate_out_kernel(place_ref, *refs):
    tokens, own, windows, (own_ref, other_ref) = refs[:8], refs[8], refs[9:13], refs[13:15]
    kept_own, kept_other, kept_tokens, sems = refs[15:17], refs[17:19], refs[19:21], refs[21]
    copies = []
    for i in range(2):
        rows = [pl.multiple_of(place_ref[2 + 2 * i + j], 16) for j in range(2)]
        for start, size in CUTS[i]:
            lanes = slice(start, start + size)
            offset = pl.multiple_of(place_ref[i] + start, 128)
            group = [(own.at[:, pl.ds(offset, size)], kept_own[i].at[:, lanes])]
            for j in range(2):
                target = kept_other[i].at[pl.ds(rows[j], 176), lanes]
                group.append((windows[2 * i + j].at[:, lanes], target))
            for half in range(2):
                for piece in range(4):
                    target = kept_tokens[i].at[
                        half * 2 : half * 2 + 2, piece * 32 : piece * 32 + 32, lanes
                    ]
                    source = tokens[half * 4 + piece].at[:, :, pl.ds(offset, size)]
                    group.append((source, target))
            copies.append(
                (
                    i,
                    lanes,
                    [
                        pltpu.make_async_copy(source, target, sems.at[11 * len(copies) + j])
                        for j, (source, target) in enumerate(group)
                    ],
                )
            )
    for _, _, group in copies:
        for copy in group:
            copy.start()
    total = [None, None]
    for i, lanes, group in copies:
        for copy in group:
            copy.wait()
        size = lanes.stop - lanes.start
        basis = jnp.concatenate([kept_other[i][:, lanes], kept_own[i][:, lanes]], 0)
        for half in range(2):
            part = lax.dot_general(
                basis,
                kept_tokens[i][half * 2 : half * 2 + 2, :, lanes].reshape(256, size),
                (((1,), (1,)), ((), ())),
                preferred_element_type=jnp.float32,
            )
            total[half] = part if total[half] is None else total[half] + part
    swap = place_ref[6] == 0
    for half in range(2):
        lanes = slice(half * 256, half * 256 + 256)
        own_ref[:, lanes] = total[half][352:].astype(own_ref.dtype)
        low, high = total[half][:176], total[half][176:352]
        rows = jnp.concatenate([jnp.where(swap, low, high), jnp.where(swap, high, low)[8:]], 0)
        other_ref[:, lanes] = rows.astype(other_ref.dtype)


def rotate_out(places, tokens, own, windows):
    shape = jax.ShapeDtypeStruct((344, 512), jnp.bfloat16)
    anywhere = pl.BlockSpec(memory_space=pltpu.HBM)
    vmem = pl.BlockSpec(memory_space=pltpu.VMEM)
    return pl.pallas_call(
        rotate_out_kernel,
        out_shape=(shape, shape),
        in_specs=[pl.BlockSpec(memory_space=pltpu.SMEM)]
        + ([anywhere] * 3 + [vmem]) * 2
        + [anywhere] * 5,
        out_specs=(vmem, vmem),
        scratch_shapes=[pltpu.VMEM((344, 5504), jnp.bfloat16)] * 2
        + [pltpu.VMEM((352, 5504), jnp.bfloat16)] * 2
        + [pltpu.VMEM((4, 128, 5504), jnp.bfloat16)] * 2
        + [pltpu.SemaphoreType.DMA((66,))],
        compiler_params=pltpu.CompilerParams(vmem_limit_bytes=ROOM),
        cost_estimate=pl.CostEstimate(
            flops=2 * 512 * 696 * 11008, bytes_accessed=(512 + 696) * 22016, transcendentals=0
        ),
        name="rotate_out",
    )(places, *tokens, own, *windows)


def product_kernel(place_ref, *refs):
    lefts, sources, (keep_ref, give_ref) = refs[:4], refs[4:8], refs[8:10]
    rights, sems = refs[10:14], refs[14]
    copies = [pltpu.make_async_copy(sources[i], rights[i], sems.at[i]) for i in range(4)]
    for i in (0, 2, 1, 3):
        copies[i].start()

    def left(half, group, example):
        lane = (half * 2 + example) * 128
        pair = [lefts[group * 2 + i] for i in range(2)]
        return jnp.concatenate([r[:, lane : lane + 128] for r in pair], 1)

    def right(half, piece, example):
        ref = rights[half * 2 + piece // 8]
        tiles = []
        for side in range(2):
            for u in range(8):
                row = side * 128 + (u ^ (piece >> 1)) * 16
                tiles.append(ref[piece % 8, example, row : row + 16, :])
        return jnp.concatenate(tiles, 0)

    for first, arrived in ((0, (0, 2)), (8, (1,)), (2, (3,)), (10, ())):
        for i in arrived:
            copies[i].wait()
        blocks = (first, first + 1, first + 4, first + 5)
        total = None
        for half in range(2):
            pieces = [s if half == 0 else (s % 4) * 4 + s // 4 for s in blocks]
            for group in range(2):
                for example in range(2):
                    rhs = jnp.concatenate(
                        [right(half, piece, group * 2 + example) for piece in pieces], 1
                    )
                    product = jnp.dot(
                        left(half, group, example), rhs, preferred_element_type=jnp.float32
                    )
                    square = product * product
                    total = square if total is None else total + square
        total = total * (1.0 / 16.0)
        for i, s in enumerate(blocks):
            place = place_ref[s]
            column = pl.multiple_of(lax.rem(place, 8) * 128, 128)
            part = total[:, i * 128 : (i + 1) * 128]

            @pl.when(place < 8)
            def _(part=part, column=column):
                keep_ref[:, pl.ds(column, 128)] = part

            @pl.when(place >= 8)
            def _(part=part, column=column):
                give_ref[:, pl.ds(column, 128)] = part


def product(places, lefts, rights):
    rows = lefts[0].shape[0]
    shape = jax.ShapeDtypeStruct((rows, 1024), jnp.float32)
    vmem = pl.BlockSpec(memory_space=pltpu.VMEM)
    return pl.pallas_call(
        product_kernel,
        out_shape=(shape, shape),
        in_specs=[pl.BlockSpec(memory_space=pltpu.SMEM)] + [vmem] * 4 + [pl.BlockSpec(memory_space=pl.ANY)] * 4,
        out_specs=(vmem, vmem),
        scratch_shapes=[pltpu.VMEM(rights[0].shape, jnp.bfloat16)] * 4
        + [pltpu.SemaphoreType.DMA((4,))],
        compiler_params=pltpu.CompilerParams(vmem_limit_bytes=24 * 1024 * 1024),
        cost_estimate=pl.CostEstimate(
            flops=2 * 8 * 256 * rows * 2048, bytes_accessed=14_000_000, transcendentals=0
        ),
        name="squares",
    )(places, *lefts, *rights)


def per_device(acts, grads, basis_in, basis_out):
    core, zl, zh = lax.axis_index("c"), lax.axis_index("zl"), lax.axis_index("zh")
    y, x = lax.axis_index("y"), lax.axis_index("x")
    steps = [steps_of(half) for half in range(2)]
    halves = range(2)

    def moved(v, step, *others):
        return [steps[half][step](after(v[half], *others) if others else v[half]) for half in halves]

    def joined(v, w, axis):
        return [jnp.concatenate([v[half], w[half]], axis) for half in halves]

    basis_out = basis_out.T

    g0 = [grads[2 * half : 2 * half + 2] for half in halves]
    a0 = [acts[2 * half : 2 * half + 2] for half in halves]
    a1 = joined(a0, moved(a0, 0), 1)
    part = flip_both(lax.dynamic_slice_in_dim(basis_in, 2048 * (1 - zl), 2048, 0))
    other_in = part, flip_zl(part)
    window = lax.dynamic_slice(basis_out, (168 * (1 - zl), 5504 * core), (176, 5504))
    g1 = joined(g0, moved(g0, 0), 1)
    a2 = joined(a1, moved(a1, 1), 1)
    first = relay(after(window, part), ("both", None))
    g2 = joined(g1, moved(g1, 1), 1)
    a3 = joined(a2, moved(a2, 2), 1)
    a4 = moved(a3, 3)

    flag = jnp.stack([(zh == zl).astype(jnp.int32), zl.astype(jnp.int32)])
    acts_pieces = [a3[0], a4[0], a3[1], a4[1]]
    keep, give = rotate_in(after(flag, first, *g2), acts_pieces, basis_in, other_in)
    keep, give = keep.reshape(4, 128, 128), give.reshape(4, 128, 128)
    exchanged = flip_zh(keep), flip_zl(give), flip_both(give)
    g3 = moved(g2, 2, a4[0])
    g4 = moved(g2, 3)
    near = jnp.concatenate([after(keep, *g3), exchanged[0]], 1)
    far = jnp.concatenate(after(exchanged[1:], *g3), 1)

    c0 = [
        jnp.concatenate([near[2 * half : 2 * half + 2], far[2 * half : 2 * half + 2]], 0)
        for half in halves
    ]
    swapped = [v.reshape(4, 16, 2, 8, 128)[:, :, ::-1].reshape(4, 256, 128) for v in c0]
    c1 = [jnp.stack([c0[half], v]) for half, v in enumerate(moved(swapped, 0))]
    second = relay(after(jnp.where(core == 0, first, window), *exchanged), ("zl", "both"))
    third = relay(after(second, *c1, *g4), (None, "zl"))

    c2 = joined(c1, moved(c1, 1), 0)
    g5 = moved(g3, 3, g4[0])
    grads_pieces = [v[half] for half in halves for v in (g2, g3, g4, g5)]
    c3 = joined(c2, moved(c2, 2), 0)
    c4 = moved(c3, 3, *g5)
    outer = jnp.where(core == 0, first, third)
    places = [5504 * core, 5504 * (1 - core)]
    places += [176 * core, 176 * (1 - core), 176 * core, 176 * (1 - core), zl]
    windows = [outer, second, flip_core(after(second, *c2)), flip_core(after(outer, *c2))]
    places = after(jnp.stack(places).astype(jnp.int32), *c3)
    mine, theirs = rotate_out(places, grads_pieces, basis_out, windows)
    rights = [v[half] for half in halves for v in (c3, c4)]
    lefts = [mine, flip_zh(theirs), flip_zl(mine), flip_both(theirs)]

    low, high = jnp.where(core == 0, 1, 3), jnp.where(core == 0, 3, 1)

    def mask(bits):
        return (low if bits & 1 else 0) ^ (high if bits & 2 else 0)

    places = jnp.stack(
        [((y ^ mask(s // 4)) * 4 + (x ^ mask(s % 4))) ^ (core * 8) for s in range(16)]
    ).astype(jnp.int32)
    keep, give = product(places, lefts, rights)
    return keep + flip_core(give)


def solution(mesh):
    fine = Mesh(mesh.devices.reshape(2, 2, 2, 4, 4), AXES)
    dp, eig = ("zl", "c"), ("zh", "y", "x")
    placed = (P(dp, eig, None), P(dp, eig, None), P(None, eig), P(None, eig))
    return jax.shard_map(
        per_device, mesh=fine, in_specs=placed, out_specs=P(eig, dp), check_vma=False
    )
```
